256 devices in a mesh: expert: 32 (over z, y), dp: 8 (over x, core).
Axes of the slice: x: 4, y: 4, z: 8, core: 2. Of those that a mesh axis runs over, the one named last changes fastest.
Arguments:
- tokens: bfloat16 [65792, 1664], P(('expert', 'dp')), may hold values from -100 to 100
- upstream: bfloat16 [65792, 1664], P(('expert', 'dp')), may hold values from -6 to 6
- gate_values: float32 [65792, 2], P(('expert', 'dp')), may hold values from 0.2 to 1
- expert_index: int32 [65792, 2], P(('expert', 'dp')), may hold values from 0 to 31, as said below
- slot_index: int32 [65792, 2], P(('expert', 'dp')), may hold values from 0 to 3, as said below
- kept_mask: int32 [65792, 2], P(('expert', 'dp')), may hold values from 0 to 1, as said below
- counts: int32 [256, 32], P(('expert', 'dp')), may hold values from 0 to 4, as said below
- norm_gain: float32 [1664], replicated, may hold values from 0.1 to 1.9
- norm_bias: float32 [1664], replicated, may hold values from -3 to 3
- in_weight: bfloat16 [32, 1664, 4096], P('expert', None, 'dp'), may hold values from -0.15625 to 0.15625
- out_weight: bfloat16 [32, 4096, 1664], P('expert', 'dp'), may hold values from -0.09375 to 0.09375
Outputs:
- mixed_out: bfloat16 [65792, 1664], P(('expert', 'dp'))
- grad_in: bfloat16 [65792, 1664], P(('expert', 'dp'))
- grad_in_weight: bfloat16 [32, 1664, 4096], P('expert', None, 'dp')
- grad_out_weight: bfloat16 [32, 4096, 1664], P('expert', 'dp')
The draws below stay inside these ranges and needn't reach their ends.
Inputs may be any that keep to these rules, and one draw needn't show every extreme that they name: `expert_index`: A token's two choices name different experts. Some expert is the first choice of the 5 highest-priority tokens of every device. `slot_index`: each device serves its choices in one priority order of its tokens, all first choices before any second choice; a kept choice's slot counts the earlier choices of that device for the same expert, so the kept slots of one device and expert are distinct and run from 0 upward. A dropped choice has slot 0. `kept_mask`: 1 exactly where the choice's rank for its expert on its device is under 4; every device drops some choice. `counts`: at most the number of kept choices of the device for the expert, and below it for some devices and experts.
All inputs are finite; a program needn't handle non-finite values.
Results may differ from the reference program's by a relative error of at most 0.0068.
Values may be sent and summed in bfloat16 or wider, within the bound.
No kernel may reach another device: no remote copies, remote signals or barrier semaphores. Data moves between devices by JAX's collectives and lax.ppermute only.
A program may use at most 128 MiB of HBM per device.

```python
import jax
import jax.numpy as jnp
from jax import lax

D = 1664
FFW = 4096
CAP = 4
TOK_DEV = 257
EXPERTS = 32
TOKENS = 65792
N_DP = 8


def shuffle_one(subkey):
    return jax.random.permutation(subkey, TOK_DEV).astype(jnp.int32)


def routing(key):
    sources = TOKENS // TOK_DEV
    busy_expert = jax.random.randint(jax.random.fold_in(key, 101), (), 0, EXPERTS, dtype=jnp.int32)
    first_draw = jax.random.randint(jax.random.fold_in(key, 102), (sources, TOK_DEV), 0, EXPERTS, dtype=jnp.int32)
    second_draw = jax.random.randint(jax.random.fold_in(key, 103), (sources, TOK_DEV), 0, EXPERTS, dtype=jnp.int32)
    offsets = jax.random.randint(jax.random.fold_in(key, 104), (sources, 1), 0, EXPERTS, dtype=jnp.int32)
    first_choice = (jnp.minimum(first_draw, second_draw) + offsets) % EXPERTS
    order_keys = jax.random.split(jax.random.fold_in(key, 105), sources)
    priority = jax.vmap(shuffle_one)(order_keys)
    row_ids = jnp.arange(sources, dtype=jnp.int32)[:, None]
    first_choice = first_choice.at[row_ids, priority[:, :CAP + 1]].set(busy_expert)
    step_sizes = jax.random.randint(jax.random.fold_in(key, 106), (sources, TOK_DEV), 1, EXPERTS, dtype=jnp.int32)
    second_choice = (first_choice + step_sizes) % EXPERTS
    first_sorted = jnp.take_along_axis(first_choice, priority, axis=1)
    second_sorted = jnp.take_along_axis(second_choice, priority, axis=1)
    labels = jnp.arange(EXPERTS, dtype=jnp.int32)
    first_hot = (first_sorted[:, :, None] == labels).astype(jnp.int32)
    second_hot = (second_sorted[:, :, None] == labels).astype(jnp.int32)
    first_run = jnp.cumsum(first_hot, axis=1)
    second_run = jnp.cumsum(second_hot, axis=1) + first_run[:, -1:, :]
    first_slot = jnp.sum(first_hot * first_run, axis=-1) - 1
    second_slot = jnp.sum(second_hot * second_run, axis=-1) - 1
    slots = jnp.zeros((sources, TOK_DEV, 2), jnp.int32)
    slots = slots.at[row_ids, priority, 0].set(first_slot)
    slots = slots.at[row_ids, priority, 1].set(second_slot)
    kept_flags = (slots < CAP).astype(jnp.int32)
    slots = jnp.where(kept_flags == 1, slots, 0).astype(jnp.int32)
    chosen = jnp.stack([first_choice, second_choice], axis=-1)
    totals = second_run[:, -1, :]
    cut_flags = (jax.random.randint(jax.random.fold_in(key, 107), (sources, EXPERTS), 0, 4, dtype=jnp.int32) == 0) & (labels[None, :] != busy_expert)
    cut_sizes = jax.random.randint(jax.random.fold_in(key, 108), (sources, EXPERTS), 1, 3, dtype=jnp.int32)
    counts = jnp.maximum(jnp.minimum(totals, CAP) - jnp.where(cut_flags, cut_sizes, 0), 0).astype(jnp.int32)
    return (chosen.reshape(TOKENS, 2), slots.reshape(TOKENS, 2), kept_flags.reshape(TOKENS, 2), counts)


def draw_expert_index(key, part):
    shared = routing(key)
    return shared[0]


def draw_slot_index(key, part):
    shared = routing(key)
    return shared[1]


def draw_kept_mask(key, part):
    shared = routing(key)
    return shared[2]


def draw_counts(key, part):
    shared = routing(key)
    return shared[3]


def draw_tokens(key, part):
    key = jax.random.fold_in(key, 11)
    base_key, column_key, token_key = jax.random.split(key, 3)
    base = jnp.clip(jax.random.normal(base_key, (TOKENS, D), jnp.float32), -6.0, 6.0)
    column_scale = jnp.exp(jax.random.uniform(column_key, (1, D), jnp.float32, -1.15, 1.15))
    token_scale = jnp.exp(jax.random.uniform(token_key, (TOKENS, 1), jnp.float32, -1.15, 1.15))
    return (base * column_scale * token_scale).astype(jnp.bfloat16)


def levels(own_key, extent, shards, least, high):
    loudness = 1.0
    for position, shards_of in shards:
        heights = jax.random.uniform(jax.random.fold_in(jax.random.fold_in(own_key, 6), position), (shards_of,), jnp.float32, least / len(shards), high / len(shards))
        loudness = loudness * jnp.repeat(jnp.exp(heights), extent[position] // shards_of).reshape((-1,) + (1,) * (len(extent) - 1 - position))
    return loudness


def centred(stream_key, dims, scale, bound, cuts=(), kind=jnp.bfloat16):
    result = jax.random.normal(stream_key, dims, jnp.float32) * scale
    if len(cuts) > 0:
        result = levels(stream_key, dims, cuts, -0.22, 0.18) * result
    return jnp.clip(result, min=-bound, max=bound).astype(kind)


def setup_inputs(seed: int = 0) -> dict:
    splits = jax.random.split(jax.random.key(seed), 12)
    return {
        "tokens": draw_tokens(jax.random.fold_in(splits[11], 71), 0),
        "upstream": centred(splits[1], (TOKENS, D), 1.0, 6.0, ((0, 256),)),
        "gate_values": jnp.clip(0.2 + 0.8 * jax.random.uniform(splits[2], (TOKENS, 2), jnp.float32) ** levels(splits[2], (TOKENS, 2), ((0, 256),), -0.2, 0.2), 0.2, 1.0),
        "expert_index": draw_expert_index(jax.random.fold_in(splits[11], 71), 0),
        "slot_index": draw_slot_index(jax.random.fold_in(splits[11], 71), 0),
        "kept_mask": draw_kept_mask(jax.random.fold_in(splits[11], 71), 0),
        "counts": draw_counts(jax.random.fold_in(splits[11], 71), 0),
        "norm_gain": jnp.clip(1.0 + 0.18 * jax.random.normal(splits[7], (D,), jnp.float32), 0.1, 1.9),
        "norm_bias": centred(splits[8], (D,), 0.5, 3.0, (), jnp.float32),
        "in_weight": centred(splits[9], (EXPERTS, D, FFW), D ** -0.5, 0.15625, ((0, 32), (2, 8))),
        "out_weight": centred(splits[10], (EXPERTS, FFW, D), FFW ** -0.5, 0.09375, ((0, 32), (1, 8))),
    }


EPSILON = 1e-06

def rounded(values):
    return lax.optimization_barrier(values.astype(jnp.bfloat16)).astype(jnp.float32)

def standardize(tokens):
    floats = tokens.astype(jnp.float32)
    center = lax.optimization_barrier(jnp.mean(floats, axis=-1, keepdims=True))
    spread = lax.optimization_barrier(jnp.mean(jnp.square(floats - center), axis=-1, keepdims=True))
    inv_std = lax.rsqrt(spread + EPSILON)
    return ((floats - center) * inv_std, inv_std)

def gelu_tanh(values):
    return jax.nn.gelu(values, approximate=True)

def expert_pass(normed_rows, gated_rows, in_matrix, out_matrix, groups):
    preact = jnp.dot(normed_rows, in_matrix, preferred_element_type=jnp.float32)
    activated = gelu_tanh(preact).astype(jnp.bfloat16)
    grad_hidden = lax.dot_general(gated_rows, out_matrix, (((1,), (1,)), ((), ())), preferred_element_type=jnp.float32)
    unused_value, pullback = jax.vjp(gelu_tanh, preact)
    grad_preact = pullback(grad_hidden)[0].astype(jnp.bfloat16)
    group_width = in_matrix.shape[1] // groups
    expert_out = jnp.zeros((normed_rows.shape[0], in_matrix.shape[0]), jnp.float32)
    back_rows = jnp.zeros((normed_rows.shape[0], in_matrix.shape[0]), jnp.float32)
    for group_index in range(groups):
        first_col = group_index * group_width
        last_col = first_col + group_width
        expert_out = expert_out + rounded(jnp.dot(activated[:, first_col:last_col], out_matrix[first_col:last_col], preferred_element_type=jnp.float32))
        back_rows = back_rows + rounded(lax.dot_general(grad_preact[:, first_col:last_col], in_matrix[:, first_col:last_col], (((1,), (1,)), ((), ())), preferred_element_type=jnp.float32))
    grad_first = lax.dot_general(normed_rows, grad_preact, (((0,), (0,)), ((), ())), preferred_element_type=jnp.float32)
    grad_second = lax.dot_general(activated, gated_rows, (((0,), (0,)), ((), ())), preferred_element_type=jnp.float32)
    return (expert_out.astype(jnp.bfloat16), back_rows.astype(jnp.bfloat16), grad_first.astype(jnp.bfloat16), grad_second.astype(jnp.bfloat16))

def reference(tokens, upstream, gate_values, expert_index, slot_index, kept_mask, counts, norm_gain, norm_bias, in_weight, out_weight):
    sources = TOKENS // TOK_DEV
    standard, inv_std = standardize(tokens)
    normed = (standard * norm_gain + norm_bias).astype(jnp.bfloat16)
    gated_grad = (gate_values[:, :, None] * upstream.astype(jnp.float32)[:, None, :]).astype(jnp.bfloat16)
    source = jnp.arange(TOKENS, dtype=jnp.int32) // TOK_DEV
    allowed = counts[source[:, None], expert_index]
    active = (kept_mask == 1) & (slot_index < allowed)
    total_slots = sources * EXPERTS * CAP
    target = (source[:, None] * EXPERTS + expert_index) * CAP + slot_index
    target = jnp.where(active, target, total_slots).astype(jnp.int32)
    flat_target = target.reshape(-1)
    normed_buffer = jnp.zeros((total_slots, D), jnp.bfloat16).at[flat_target].set(jnp.repeat(normed, 2, axis=0), mode='drop')
    gated_buffer = jnp.zeros((total_slots, D), jnp.bfloat16).at[flat_target].set(gated_grad.reshape(-1, D), mode='drop')

    def by_expert(buffer):
        return buffer.reshape(sources, EXPERTS, CAP, D).transpose(1, 0, 2, 3).reshape(EXPERTS, sources * CAP, D)

    def by_source(buffer):
        return buffer.reshape(EXPERTS, sources, CAP, D).transpose(1, 0, 2, 3).reshape(total_slots, D)

    def one_expert(operands):
        return expert_pass(operands[0], operands[1], operands[2], operands[3], N_DP)
    expert_out, back_rows, grad_in_weight, grad_out_weight = lax.map(one_expert, (by_expert(normed_buffer), by_expert(gated_buffer), in_weight, out_weight))
    fetch_rows = jnp.clip(target, 0, total_slots - 1)
    weights = jnp.where(active, gate_values, 0.0)
    active_float = jnp.where(active, 1.0, 0.0).astype(jnp.float32)
    combined = by_source(expert_out)
    mixed_out = tokens.astype(jnp.float32)
    mixed_out = mixed_out + weights[:, 0, None] * combined[fetch_rows[:, 0]].astype(jnp.float32)
    mixed_out = mixed_out + weights[:, 1, None] * combined[fetch_rows[:, 1]].astype(jnp.float32)
    back_sums = by_source(back_rows)
    back_norm = active_float[:, 0, None] * back_sums[fetch_rows[:, 0]].astype(jnp.float32)
    back_norm = back_norm + active_float[:, 1, None] * back_sums[fetch_rows[:, 1]].astype(jnp.float32)
    scaled = back_norm * norm_gain
    grad_in = upstream.astype(jnp.float32) + inv_std * (scaled - lax.optimization_barrier(jnp.mean(scaled, axis=-1, keepdims=True)) - standard * lax.optimization_barrier(jnp.mean(scaled * standard, axis=-1, keepdims=True)))
    return (mixed_out.astype(jnp.bfloat16), grad_in.astype(jnp.bfloat16), grad_in_weight, grad_out_weight)
```

```python
import functools

import jax
import jax.numpy as jnp
from jax import lax
from jax.experimental import pallas as pl
from jax.experimental.pallas import tpu as pltpu
from jax.sharding import PartitionSpec as P

CAP = 4
EPSILON = 1e-06
VMEM = pl.BlockSpec(memory_space=pltpu.VMEM)
SMEM = pl.BlockSpec(memory_space=pltpu.SMEM)
MIB = 1024 * 1024
F32 = jnp.float32
BF16 = jnp.bfloat16


def call(kernel, outs, ins, flops=0, limit=32, name=None):
    moved = sum(a.size * a.dtype.itemsize for a in list(outs) + [i for i, _ in ins])
    return pl.pallas_call(
        kernel,
        out_shape=[jax.ShapeDtypeStruct(o.shape, o.dtype) for o in outs],
        in_specs=[spec for _, spec in ins],
        out_specs=[VMEM] * len(outs),
        compiler_params=pltpu.CompilerParams(vmem_limit_bytes=limit * MIB),
        cost_estimate=pl.CostEstimate(flops=flops, bytes_accessed=moved, transcendentals=0),
        name=name,
    )(*[i for i, _ in ins])


def sds(shape, dtype):
    return jax.ShapeDtypeStruct(shape, dtype)


def standardize(floats):
    center = jnp.mean(floats, axis=-1, keepdims=True)
    spread = jnp.mean(jnp.square(floats - center), axis=-1, keepdims=True)
    inv_std = lax.rsqrt(spread + EPSILON)
    return (floats - center) * inv_std, inv_std


def one_hots(target, slots):
    rows = lax.broadcasted_iota(jnp.int32, (slots, target.shape[1]), 0)
    return rows == target[0:1], rows == target[1:2]


def dispatch_kernel(counts, tokens, upstream, gates, expert, slot, kept, gain, bias, x_out, g_out, t_out):
    experts = counts.shape[1]
    slots = experts * CAP
    standard, _ = standardize(tokens[...].astype(F32))
    normed = (standard * gain[...] + bias[...]).astype(BF16)
    chosen = expert[...]
    allowed = jnp.zeros(chosen.shape, jnp.int32)
    for e in range(experts):
        allowed = jnp.where(chosen == e, counts[0, e], allowed)
    active = (kept[...] == 1) & (slot[...] < allowed)
    target = jnp.where(active, chosen * CAP + slot[...], slots)
    t_out[...] = target
    first, second = one_hots(target, slots)
    pick = jnp.where(first | second, 1.0, 0.0).astype(BF16)
    gate = jnp.where(first, gates[0:1], 0.0) + jnp.where(second, gates[1:2], 0.0)
    gate = jnp.sum(gate, axis=1, keepdims=True)
    x_out[...] = jnp.dot(pick, normed, preferred_element_type=F32).astype(BF16)
    g_out[...] = (gate * jnp.dot(pick, upstream[...], preferred_element_type=F32)).astype(BF16)


def gather_rows(refs, out):
    at = 0
    for ref in refs:
        out[pl.ds(at, ref.shape[0]), :] = ref[...]
        at += ref.shape[0]


def forward_kernel(x0, x1, x2, x3, x4, in_a, in_b, out_a, out_b, x_all, act_a, act_b, slope_a, slope_b, own, others):
    gather_rows((x0, x1, x2, x3, x4), x_all)
    rows = x0.shape[0]
    c = 0.7978845608028654
    total = None
    for w_in, w_out, act, slope in ((in_a, out_a, act_a, slope_a), (in_b, out_b, act_b, slope_b)):
        v = jnp.dot(x_all[...], w_in[...], preferred_element_type=F32)
        square = v * v
        t = jnp.tanh(c * v * (1.0 + 0.044715 * square))
        act[...] = (0.5 * v * (1.0 + t)).astype(BF16)
        slope[...] = 0.5 * (1.0 + t) + 0.5 * v * (1.0 - t * t) * (c * (1.0 + 3 * 0.044715 * square))
        term = jnp.dot(act[...], w_out[...], preferred_element_type=F32)
        total = term if total is None else total + term
    own[...] = total[:rows]
    others[...] = total[rows:].astype(BF16)


def backward_kernel(g0, g1, g2, g3, g4, in_a, in_b, out_a, out_b, slope_a, slope_b, g_all, grad_a, grad_b, own, others):
    gather_rows((g0, g1, g2, g3, g4), g_all)
    rows = g0.shape[0]
    total = None
    nt = (((1,), (1,)), ((), ()))
    for w_in, w_out, slope, grad in ((in_a, out_a, slope_a, grad_a), (in_b, out_b, slope_b, grad_b)):
        hidden = lax.dot_general(g_all[...], w_out[...], nt, preferred_element_type=F32)
        grad[...] = (hidden * slope[...]).astype(BF16)
        term = lax.dot_general(grad[...], w_in[...], nt, preferred_element_type=F32)
        total = term if total is None else total + term
    own[...] = total[:rows]
    others[...] = total[rows:].astype(BF16)


TN = (((0,), (0,)), ((), ()))


def weight_kernel(x_all, grad, act, g_all, first, second):
    first[...] = lax.dot_general(x_all[...], grad[...], TN, preferred_element_type=F32).astype(BF16)
    second[...] = lax.dot_general(act[...], g_all[...], TN, preferred_element_type=F32).astype(BF16)


def weight_sum_kernel(x_all, grad, act, g_all, more_first, more_second, first, second):
    total = lax.dot_general(x_all[...], grad[...], TN, preferred_element_type=F32)
    first[...] = (total + more_first[...].astype(F32)).astype(BF16)
    total = lax.dot_general(act[...], g_all[...], TN, preferred_element_type=F32)
    second[...] = (total + more_second[...].astype(F32)).astype(BF16)


def mix_kernel(tokens, target, gates, rows, out):
    first, second = one_hots(target[...], rows.shape[0])
    weight = jnp.where(first, gates[0:1], 0.0) + jnp.where(second, gates[1:2], 0.0)
    total = tokens[...].astype(F32)
    for _ in range(3):
        part = weight.astype(BF16)
        weight = weight - part.astype(F32)
        total = total + lax.dot_general(part, rows[...], TN, preferred_element_type=F32)
    out[...] = total.astype(BF16)


def input_grad_kernel(tokens, upstream, target, gain, rows, out):
    first, second = one_hots(target[...], rows.shape[0])
    pick = jnp.where(first | second, 1.0, 0.0).astype(BF16)
    back = lax.dot_general(pick, rows[...], TN, preferred_element_type=F32)
    scaled = back * gain[...]
    standard, inv_std = standardize(tokens[...].astype(F32))
    inner = jnp.mean(scaled * standard, axis=-1, keepdims=True)
    centred = scaled - jnp.mean(scaled, axis=-1, keepdims=True) - standard * inner
    out[...] = (upstream[...].astype(F32) + inv_std * centred).astype(BF16)


def on_device(n_dp, tokens, upstream, gates, expert, slot, kept, counts, gain, bias, in_weight, out_weight):
    experts = counts.shape[1]
    slots = experts * CAP
    n_tok, features = tokens.shape
    in_a, out_a = in_weight[0], out_weight[0]
    hidden = in_a.shape[1]
    half = slots // 2
    n_rows = slots * n_dp // 2
    right = [(i, (i + 2) % n_dp) for i in range(n_dp)]
    left = [(i, (i - 2) % n_dp) for i in range(n_dp)]
    sibling = [(i, i ^ 1) for i in range(n_dp)]

    def send(array, pairs):
        return lax.ppermute(array, "dp", pairs)

    def exchange(rows):
        split = rows.reshape(experts, CAP, features)
        return lax.all_to_all(split, "expert", 0, 0, tiled=True).reshape(slots, features)

    def ring_gather(rows):
        top, bottom = rows[:half], rows[half:]
        from_right = send(top, left)
        from_left = send(bottom, right)
        from_right_bottom = send(bottom, left)
        from_left_top = send(top, right)
        far_top = send(from_right, left)
        far_bottom = send(from_left, right)
        near_right = jnp.concatenate([from_right, from_right_bottom], 0)
        near_left = jnp.concatenate([from_left_top, from_left], 0)
        return rows, near_right, near_left, far_top, far_bottom

    def ring_sum(own, others):
        pr, pl_ = others[:slots], others[slots : 2 * slots]
        ft, fb = others[2 * slots : 2 * slots + half], others[2 * slots + half :]
        a_top = send(ft, right)
        a_bot = send(fb, left)
        r_bot = send(pr[half:], right)
        l_top = send(pl_[:half], left)
        r_top = send((pr[:half].astype(F32) + a_top.astype(F32)).astype(BF16), right)
        l_bot = send((pl_[half:].astype(F32) + a_bot.astype(F32)).astype(BF16), left)
        top = own[:half] + r_top.astype(F32) + l_top.astype(F32)
        bottom = own[half:] + r_bot.astype(F32) + l_bot.astype(F32)
        return jnp.concatenate([top, bottom], 0).astype(BF16)

    gates_t, expert_t, slot_t, kept_t = gates.T, expert.T, slot.T, kept.T
    gain, bias = gain[None], bias[None]
    x, g, target = call(
        dispatch_kernel,
        [sds((slots, features), BF16), sds((slots, features), BF16), sds((2, n_tok), jnp.int32)],
        [(counts, SMEM)] + [(a, VMEM) for a in (tokens, upstream, gates_t, expert_t, slot_t, kept_t, gain, bias)],
        flops=4 * slots * n_tok * features,
        name="dispatch",
    )
    in_b, out_b = send(in_a, sibling), send(out_a, sibling)
    x_blocks = ring_gather(exchange(x))
    g_blocks = ring_gather(exchange(g))
    wide, narrow = sds((n_rows, features), BF16), sds((n_rows, hidden), BF16)
    slope = sds((n_rows, hidden), F32)
    own, others = sds((slots, features), F32), sds((n_rows - slots, features), BF16)
    flops = 8 * n_rows * features * hidden
    weights = (in_a, in_b, out_a, out_b)
    x_all, act_a, act_b, slope_a, slope_b, own_out, out = call(
        forward_kernel,
        [wide, narrow, narrow, slope, slope, own, others],
        [(a, VMEM) for a in x_blocks + weights],
        flops=flops,
        limit=48,
        name="forward",
    )
    g_all, grad_a, grad_b, own_back, back = call(
        backward_kernel,
        [wide, narrow, narrow, own, others],
        [(a, VMEM) for a in g_blocks + weights + (slope_a, slope_b)],
        flops=flops,
        limit=48,
        name="backward",
    )
    first, second = sds(in_a.shape, BF16), sds(out_a.shape, BF16)
    first_b, second_b = call(
        weight_kernel,
        [first, second],
        [(a, VMEM) for a in (x_all, grad_b, act_b, g_all)],
        flops=flops // 2,
        limit=48,
        name="weights_b",
    )
    more_first, more_second = send(first_b, sibling), send(second_b, sibling)
    home_out = exchange(ring_sum(own_out, out))
    (mixed,) = call(
        mix_kernel,
        [sds(tokens.shape, BF16)],
        [(a, VMEM) for a in (tokens, target, gates_t, home_out)],
        flops=6 * slots * n_tok * features,
        name="mix",
    )
    home_back = exchange(ring_sum(own_back, back))
    grad_first, grad_second = call(
        weight_sum_kernel,
        [first, second],
        [(a, VMEM) for a in (x_all, grad_a, act_a, g_all, more_first, more_second)],
        flops=flops // 2,
        limit=48,
        name="weights_a",
    )
    (grad_in,) = call(
        input_grad_kernel,
        [sds(tokens.shape, BF16)],
        [(a, VMEM) for a in (tokens, upstream, target, gain, home_back)],
        flops=2 * slots * n_tok * features,
        name="input_grad",
    )
    return mixed, grad_in, grad_first[None], grad_second[None]


def solution(mesh):
    rows = P(("expert", "dp"), None)
    in_specs = (rows,) * 7 + (P(), P(), P("expert", None, "dp"), P("expert", "dp", None))
    out_specs = (rows, rows, P("expert", None, "dp"), P("expert", "dp", None))
    body = functools.partial(on_device, mesh.shape["dp"])
    return jax.shard_map(body, mesh=mesh, in_specs=in_specs, out_specs=out_specs, check_vma=False)
```

```python
import functools

import jax
import jax.numpy as jnp
from jax import lax
from jax.experimental import pallas as pl
from jax.experimental.pallas import tpu as pltpu
from jax.sharding import PartitionSpec as P

CAP = 4
EPSILON = 1e-06
HBM = pl.BlockSpec(memory_space=pltpu.HBM)
VMEM = pl.BlockSpec(memory_space=pltpu.VMEM)
MIB = 1024 * 1024
F32 = jnp.float32
BF16 = jnp.bfloat16
TN = (((0,), (0,)), ((), ()))
NT = (((1,), (1,)), ((), ()))
sds = jax.ShapeDtypeStruct


def call(body, outs, ins, scalars=(), here=(), keep=(), flops=0, name=None):
    n_in, n_out, n_s = len(ins), len(outs), len(scalars)
    far_in = [i for i in range(n_in) if i not in here]
    far_out = [i for i in range(n_out) if i not in keep]

    def kernel(*refs):
        words, refs = refs[:n_s], refs[n_s:]
        source, refs = refs[:n_in], refs[n_in:]
        sink, refs = refs[:n_out], refs[n_out:]
        held, refs = dict(zip(far_in, refs)), refs[len(far_in) :]
        made, refs = dict(zip(far_out, refs)), refs[len(far_out) :]
        in_sem, out_sem, word_sem, *smem = refs
        word_copies = [pltpu.make_async_copy(a, b, word_sem.at[k]) for k, (a, b) in enumerate(zip(words, smem))]
        for c in word_copies:
            c.start()
        copies = {i: pltpu.make_async_copy(source[i], held[i], in_sem.at[k]) for k, i in enumerate(far_in)}
        for c in copies.values():
            c.start()
        for c in word_copies:
            c.wait()
        waited, sent = set(), []

        def load(i):
            if i not in copies:
                return source[i]
            if i not in waited:
                waited.add(i)
                copies[i].wait()
            return held[i]

        def store(i):
            if i in made:
                c = pltpu.make_async_copy(made[i], sink[i], out_sem.at[far_out.index(i)])
                c.start()
                sent.append(c)

        body(load, [made.get(i, sink[i]) for i in range(n_out)], store, smem)
        for c in sent:
            c.wait()

    moved = sum(a.size * a.dtype.itemsize for a in list(outs) + list(ins))
    buffers = [pltpu.VMEM(ins[i].shape, ins[i].dtype) for i in far_in]
    buffers += [pltpu.VMEM(outs[i].shape, outs[i].dtype) for i in far_out]
    sems = [pltpu.SemaphoreType.DMA((max(1, len(k)),)) for k in (far_in, far_out, scalars)]
    words = [pltpu.SMEM(a.shape, a.dtype) for a in scalars]
    scalars = [pltpu.with_memory_space_constraint(a, pltpu.HBM) for a in scalars]
    ins = [a if i in here else pltpu.with_memory_space_constraint(a, pltpu.HBM) for i, a in enumerate(ins)]
    outs = [o if i in keep else pltpu.HBM(o.shape, o.dtype) for i, o in enumerate(outs)]
    return pl.pallas_call(
        kernel,
        out_shape=outs,
        in_specs=[HBM] * n_s + [VMEM if i in here else HBM for i in range(n_in)],
        out_specs=[VMEM if i in keep else HBM for i in range(n_out)],
        scratch_shapes=buffers + sems + words,
        compiler_params=pltpu.CompilerParams(vmem_limit_bytes=36 * MIB),
        cost_estimate=pl.CostEstimate(flops=flops, bytes_accessed=moved, transcendentals=0),
        name=name,
    )(*scalars, *ins)


def after(values, *others):
    return lax.optimization_barrier((values, others))[0]


def standardize(floats):
    center = jnp.mean(floats, axis=-1, keepdims=True)
    spread = jnp.mean(jnp.square(floats - center), axis=-1, keepdims=True)
    inv_std = lax.rsqrt(spread + EPSILON)
    return (floats - center) * inv_std, inv_std


def one_hots(target, slots):
    rows = lax.broadcasted_iota(jnp.int32, (slots, target.shape[1]), 0)
    return rows == target[0:1], rows == target[1:2]


def either(first, second):
    return jnp.where(first | second, 1.0, 0.0).astype(BF16)


def weighted(first, second, gates):
    return jnp.where(first, gates[0:1], 0.0) + jnp.where(second, gates[1:2], 0.0)


def rows_of(ref, part):
    return ref[:, part].reshape(ref.shape[0] * ref.shape[2], ref.shape[3])


def dispatch(load, made, store, smem):
    (counts,) = smem
    experts = counts.shape[1]
    slots = experts * CAP
    chosen, slot, kept = load(0)[...], load(1)[...], load(2)[...]
    allowed = jnp.zeros(chosen.shape, jnp.int32)
    for e in range(experts):
        allowed = jnp.where(chosen == e, counts[0, e], allowed)
    active = (kept == 1) & (slot < allowed)
    target = jnp.where(active, chosen * CAP + slot, slots)
    made[1][...] = target
    store(1)
    first, second = one_hots(target, slots)
    pick = either(first, second)
    gate = jnp.sum(weighted(first, second, load(3)[...]), axis=1, keepdims=True)
    block = (experts, CAP, made[0].shape[3])
    rows = gate * jnp.dot(pick, load(4)[...], preferred_element_type=F32)
    made[0][:, 1] = rows.astype(BF16).reshape(block)
    standard, _ = standardize(load(5)[...].astype(F32))
    normed = (standard * load(6)[...][None] + load(7)[...][None]).astype(BF16)
    rows = jnp.dot(pick, normed, preferred_element_type=F32)
    made[0][:, 0] = rows.astype(BF16).reshape(block)
    store(0)


def expert_rows(n, load, made, store, smem):
    x_all, g_all = made[0], made[1]
    for part, out in ((0, x_all), (1, g_all)):
        at = 0
        for i in range(n):
            rows = rows_of(load(i), part)
            out[pl.ds(at, rows.shape[0]), :] = rows
            at += rows.shape[0]
        store(part)
    c = 0.7978845608028654
    out, back = None, None
    for k in range(2):
        w_in, w_out = load(n + 2 * k), load(n + 2 * k + 1)
        v = jnp.dot(x_all[...], w_in[...], preferred_element_type=F32)
        square = v * v
        t = jnp.tanh(c * v * (1.0 + 0.044715 * square))
        act, grad = made[2 + k], made[4 + k]
        act[...] = (0.5 * v * (1.0 + t)).astype(BF16)
        store(2 + k)
        slope = 0.5 * (1.0 + t) + 0.5 * v * (1.0 - t * t) * (c * (1.0 + 3 * 0.044715 * square))
        hidden = lax.dot_general(g_all[...], w_out[...], NT, preferred_element_type=F32)
        grad[...] = (hidden * slope).astype(BF16)
        store(4 + k)
        term = jnp.dot(act[...], w_out[...], preferred_element_type=F32)
        out = term if out is None else out + term
        term = lax.dot_general(grad[...], w_in[...], NT, preferred_element_type=F32)
        back = term if back is None else back + term
    at = 0
    for i in range(6, len(made)):
        ref = made[i]
        size = ref.shape[0] * CAP
        for part, total in ((0, out), (1, back)):
            piece = total[at : at + size].astype(ref.dtype)
            ref[:, part] = piece.reshape(ref.shape[0], CAP, ref.shape[3])
        store(i)
        at += size


def tall_product(load, first):
    total = None
    for i in (first, first + 2, first + 4):
        term = lax.dot_general(load(i)[...], load(i + 1)[...], TN, preferred_element_type=F32)
        total = term if total is None else total + term
    return total


def weight_grads(load, made, store, smem):
    for k in range(2):
        made[k][...] = tall_product(load, 6 * k).astype(BF16)
        store(k)


def weight_sums(load, made, store, smem):
    for k in range(2):
        made[k][...] = (tall_product(load, 6 * k) + load(12 + k)[...].astype(F32)).astype(BF16)
        store(k)


def home_sum(load, made, store, smem):
    half = made[0].shape[0] // 2
    for k in range(2):
        part = pl.ds(k * half, half)
        total = load(0)[part] + load(1 + k)[...].astype(F32) + load(3 + k)[...].astype(F32)
        made[0][part] = total.astype(BF16)
    store(0)


def combine(load, made, store, smem):
    target, gates = load(0)[...], load(1)[...]
    tokens = load(2)[...].astype(F32)
    standard, inv_std = standardize(tokens)
    home = load(5)
    first, second = one_hots(target, home.shape[0] * CAP)
    rows = rows_of(home, 0)
    weight = weighted(first, second, gates)
    total = tokens
    for _ in range(3):
        part = weight.astype(BF16)
        weight = weight - part.astype(F32)
        total = total + lax.dot_general(part, rows, TN, preferred_element_type=F32)
    made[0][...] = total.astype(BF16)
    store(0)
    back = lax.dot_general(either(first, second), rows_of(home, 1), TN, preferred_element_type=F32)
    scaled = back * load(3)[...][None]
    inner = jnp.mean(scaled * standard, axis=-1, keepdims=True)
    centred = scaled - jnp.mean(scaled, axis=-1, keepdims=True) - standard * inner
    made[1][...] = (load(4)[...].astype(F32) + inv_std * centred).astype(BF16)
    store(1)


def on_device(n_dp, tokens, upstream, gates, expert, slot, kept, counts, gain, bias, in_weight, out_weight):
    experts = counts.shape[1]
    slots = experts * CAP
    n_tok, features = tokens.shape
    in_a, out_a = in_weight[0], out_weight[0]
    hidden = in_a.shape[1]
    half = experts // 2
    n_rows = slots * n_dp // 2
    right = [(i, (i + 2) % n_dp) for i in range(n_dp)]
    left = [(i, (i - 2) % n_dp) for i in range(n_dp)]
    sibling = [(i, i ^ 1) for i in range(n_dp)]

    def send(array, pairs):
        return lax.ppermute(array, "dp", pairs)

    def exchange(rows):
        return lax.all_to_all(rows, "expert", 0, 0, tiled=True)

    def add(a, b):
        return (a.astype(F32) + b.astype(F32)).astype(BF16)

    gates_t, expert_t, slot_t, kept_t = gates.T, expert.T, slot.T, kept.T
    block = sds((experts, 2, CAP, features), BF16)
    half_block = sds((half, 2, CAP, features), BF16)
    small = 2 * slots * n_tok * features
    in_b, out_b = send(in_a, sibling), send(out_a, sibling)
    rows, target = call(
        dispatch,
        [block, sds((2, n_tok), jnp.int32)],
        [expert_t, slot_t, kept_t, gates_t, upstream, tokens, gain, bias],
        scalars=[counts],
        keep=[0],
        flops=2 * small,
        name="dispatch",
    )
    rows, in_b, out_b = lax.optimization_barrier((exchange(rows), in_b, out_b))
    from_right, from_left = send(rows, left), send(rows, right)

    def experts_of(blocks, results, name):
        n = sum(b.shape[0] for b in blocks) * CAP
        wide, narrow = sds((n, features), BF16), sds((n, hidden), BF16)
        return call(
            functools.partial(expert_rows, len(blocks)),
            [wide, wide] + [narrow] * 4 + results,
            [*blocks, in_a, out_a, in_b, out_b],
            here=range(len(blocks) + 4),
            keep=range(6, 6 + len(results)),
            flops=16 * n * features * hidden,
            name=name,
        )

    own_block = sds(block.shape, F32)
    x_own, g_own, own_act_a, own_act_b, own_grad_a, own_grad_b, own = experts_of([rows], [own_block], "own_rows")
    from_right, from_left, own = lax.optimization_barrier((from_right, from_left, own))
    far_top, far_bottom = send(from_right[:half], left), send(from_left[half:], right)
    x_near, g_near, act_a, act_b, grad_a, grad_b, right_top, right_bottom, left_top, left_bottom = experts_of(
        [from_right, from_left], [half_block] * 4, "near_rows"
    )
    far_top, far_bottom, right_bottom, left_top = lax.optimization_barrier(
        (far_top, far_bottom, right_bottom, left_top)
    )
    right_bottom, left_top = send(right_bottom, right), send(left_top, left)
    x_far, g_far, far_act_a, far_act_b, far_grad_a, far_grad_b, far_top, far_bottom = experts_of(
        [far_top, far_bottom], [half_block] * 2, "far_rows"
    )
    far_top, far_bottom = send(far_top, right), send(far_bottom, left)
    first, second = sds(in_a.shape, BF16), sds(out_a.shape, BF16)
    flops = 4 * n_rows * features * hidden
    first_b, second_b = call(
        weight_grads,
        [first, second],
        after([x_near, grad_b], right_bottom, left_top)
        + [x_far, far_grad_b, x_own, own_grad_b, act_b, g_near, far_act_b, g_far, own_act_b, g_own],
        keep=range(2),
        flops=flops,
        name="weights_b",
    )
    right_top, left_bottom, first_b, second_b = lax.optimization_barrier(
        (add(right_top, far_top), add(left_bottom, far_bottom), first_b, second_b)
    )
    right_top, left_bottom = send(right_top, right), send(left_bottom, left)
    more_first, more_second = send(first_b, sibling), send(second_b, sibling)
    parts = [own, right_top, right_bottom, left_top, left_bottom]
    (home,) = call(home_sum, [block], parts, here=range(5), keep=[0], name="home_sum")
    home = exchange(home)
    grad_first, grad_second = call(
        weight_sums,
        [first, second],
        [x_near, grad_a, x_far, far_grad_a, x_own, own_grad_a]
        + [act_a, g_near, far_act_a, g_far, own_act_a, g_own, more_first, more_second],
        here=(12, 13),
        flops=flops,
        name="weights_a",
    )
    home = after(home, grad_first)
    like = sds(tokens.shape, BF16)
    mixed, grad_in = call(
        combine,
        [like, like],
        [target, gates_t, tokens, gain, upstream, home],
        here=[5],
        flops=4 * small,
        name="combine",
    )
    return mixed, grad_in, grad_first[None], grad_second[None]


def solution(mesh):
    rows = P(("expert", "dp"), None)
    in_specs = (rows,) * 7 + (P(), P(), P("expert", None, "dp"), P("expert", "dp", None))
    out_specs = (rows, rows, P("expert", None, "dp"), P("expert", "dp", None))
    body = functools.partial(on_device, mesh.shape["dp"])
    return jax.shard_map(body, mesh=mesh, in_specs=in_specs, out_specs=out_specs, check_vma=False)
```

```python
import functools

import jax
import jax.numpy as jnp
from jax import lax
from jax.experimental import pallas as pl
from jax.experimental.pallas import tpu as pltpu
from jax.sharding import PartitionSpec as P

CAP = 4
EPSILON = 1e-06
HBM = pl.BlockSpec(memory_space=pltpu.HBM)
VMEM = pl.BlockSpec(memory_space=pltpu.VMEM)
MIB = 1024 * 1024
F32 = jnp.float32
BF16 = jnp.bfloat16
TN = (((0,), (0,)), ((), ()))
NT = (((1,), (1,)), ((), ()))
sds = jax.ShapeDtypeStruct


def call(body, outs, ins, scalars=(), here=(), keep=(), flops=0, name=None):
    n_in, n_out, n_s = len(ins), len(outs), len(scalars)
    far_in = [i for i in range(n_in) if i not in here]
    far_out = [i for i in range(n_out) if i not in keep]

    def kernel(*refs):
        words, refs = refs[:n_s], refs[n_s:]
        source, refs = refs[:n_in], refs[n_in:]
        sink, refs = refs[:n_out], refs[n_out:]
        held, refs = dict(zip(far_in, refs)), refs[len(far_in) :]
        made, refs = dict(zip(far_out, refs)), refs[len(far_out) :]
        in_sem, out_sem, word_sem, *smem = refs
        word_copies = [pltpu.make_async_copy(a, b, word_sem.at[k]) for k, (a, b) in enumerate(zip(words, smem))]
        for c in word_copies:
            c.start()
        copies = {i: pltpu.make_async_copy(source[i], held[i], in_sem.at[k]) for k, i in enumerate(far_in)}
        for c in copies.values():
            c.start()
        for c in word_copies:
            c.wait()
        waited, sent = set(), []

        def load(i):
            if i not in copies:
                return source[i]
            if i not in waited:
                waited.add(i)
                copies[i].wait()
            return held[i]

        def store(i):
            if i in made:
                c = pltpu.make_async_copy(made[i], sink[i], out_sem.at[far_out.index(i)])
                c.start()
                sent.append(c)

        body(load, [made.get(i, sink[i]) for i in range(n_out)], store, smem)
        for c in sent:
            c.wait()

    moved = sum(a.size * a.dtype.itemsize for a in list(outs) + list(ins))
    buffers = [pltpu.VMEM(ins[i].shape, ins[i].dtype) for i in far_in]
    buffers += [pltpu.VMEM(outs[i].shape, outs[i].dtype) for i in far_out]
    sems = [pltpu.SemaphoreType.DMA((max(1, len(k)),)) for k in (far_in, far_out, scalars)]
    words = [pltpu.SMEM(a.shape, a.dtype) for a in scalars]
    scalars = [pltpu.with_memory_space_constraint(a, pltpu.HBM) for a in scalars]
    ins = [a if i in here else pltpu.with_memory_space_constraint(a, pltpu.HBM) for i, a in enumerate(ins)]
    outs = [o if i in keep else pltpu.HBM(o.shape, o.dtype) for i, o in enumerate(outs)]
    return pl.pallas_call(
        kernel,
        out_shape=outs,
        in_specs=[HBM] * n_s + [VMEM if i in here else HBM for i in range(n_in)],
        out_specs=[VMEM if i in keep else HBM for i in range(n_out)],
        scratch_shapes=buffers + sems + words,
        compiler_params=pltpu.CompilerParams(vmem_limit_bytes=28 * MIB),
        cost_estimate=pl.CostEstimate(flops=flops, bytes_accessed=moved, transcendentals=0),
        name=name,
    )(*scalars, *ins)


def after(values, *others):
    return lax.optimization_barrier((values, others))[0]


def moments(floats):
    center = jnp.mean(floats, axis=-1, keepdims=True)
    spread = jnp.mean(jnp.square(floats - center), axis=-1, keepdims=True)
    return center, lax.rsqrt(spread + EPSILON)


def one_hots(target, slots):
    rows = lax.broadcasted_iota(jnp.int32, (slots, target.shape[1]), 0)
    return rows == target[0:1], rows == target[1:2]


def either(first, second):
    return jnp.where(first | second, 1.0, 0.0).astype(BF16)


def weighted(first, second, gates):
    return jnp.where(first, gates[0:1], 0.0) + jnp.where(second, gates[1:2], 0.0)


def rows_of(ref, part):
    return ref[:, part].reshape(ref.shape[0] * ref.shape[2], ref.shape[3])


def dispatch(load, made, store, smem):
    (counts,) = smem
    experts = counts.shape[1]
    slots = experts * CAP
    chosen, slot, kept = load(0)[...], load(1)[...], load(2)[...]
    allowed = jnp.zeros(chosen.shape, jnp.int32)
    for e in range(experts):
        allowed = jnp.where(chosen == e, counts[0, e], allowed)
    active = (kept == 1) & (slot < allowed)
    target = jnp.where(active, chosen * CAP + slot, slots)
    made[1][...] = target
    store(1)
    first, second = one_hots(target, slots)
    pick = either(first, second)
    gate = jnp.sum(weighted(first, second, load(3)[...]), axis=1, keepdims=True)
    block = (experts, CAP, made[0].shape[3])
    rows = gate * jnp.dot(pick, load(4)[...], preferred_element_type=F32)
    made[0][:, 1] = rows.astype(BF16).reshape(block)
    floats = load(5)[...].astype(F32)
    center, inv_std = moments(floats)
    made[2][:, 0:1] = center
    made[2][:, 1:2] = inv_std
    normed = ((floats - center) * inv_std * load(6)[...][None] + load(7)[...][None]).astype(BF16)
    rows = jnp.dot(pick, normed, preferred_element_type=F32)
    made[0][:, 0] = rows.astype(BF16).reshape(block)
    store(0)


def expert_rows(n, load, made, store, smem):
    x_all, g_all = made[0], made[1]
    for part, out in ((0, x_all), (1, g_all)):
        at = 0
        for i in range(n):
            rows = rows_of(load(i), part)
            out[pl.ds(at, rows.shape[0]), :] = rows
            at += rows.shape[0]
        store(part)
    c = 0.7978845608028654
    out, back = None, None
    for k in range(2):
        w_in, w_out = load(n + 2 * k), load(n + 2 * k + 1)
        v = jnp.dot(x_all[...], w_in[...], preferred_element_type=F32)
        square = v * v
        t = jnp.tanh(c * v * (1.0 + 0.044715 * square))
        act, grad = made[2 + k], made[4 + k]
        act[...] = (0.5 * v * (1.0 + t)).astype(BF16)
        store(2 + k)
        slope = 0.5 * (1.0 + t) + 0.5 * v * (1.0 - t * t) * (c * (1.0 + 3 * 0.044715 * square))
        hidden = lax.dot_general(g_all[...], w_out[...], NT, preferred_element_type=F32)
        grad[...] = (hidden * slope).astype(BF16)
        store(4 + k)
        term = jnp.dot(act[...], w_out[...], preferred_element_type=F32)
        out = term if out is None else out + term
        term = lax.dot_general(grad[...], w_in[...], NT, preferred_element_type=F32)
        back = term if back is None else back + term
    at = 0
    for i in range(6, len(made)):
        ref = made[i]
        size = ref.shape[0] * CAP
        for part, total in ((0, out), (1, back)):
            piece = total[at : at + size].astype(ref.dtype)
            ref[:, part] = piece.reshape(ref.shape[0], CAP, ref.shape[3])
        store(i)
        at += size


def tall_product(load, first):
    total = None
    for i in (first, first + 2, first + 4):
        term = lax.dot_general(load(i)[...], load(i + 1)[...], TN, preferred_element_type=F32)
        total = term if total is None else total + term
    return total


def weight_grads(load, made, store, smem):
    for k in range(2):
        made[k][...] = tall_product(load, 6 * k).astype(BF16)
        store(k)


def weight_sums(load, made, store, smem):
    for k in range(2):
        made[k][...] = (tall_product(load, 6 * k) + load(12 + k)[...].astype(F32)).astype(BF16)
        store(k)


def home_sum(load, made, store, smem):
    half = made[0].shape[0] // 2
    for k in range(2):
        part = pl.ds(k * half, half)
        total = load(0)[part] + load(1 + k)[...].astype(F32) + load(3 + k)[...].astype(F32)
        made[0][part] = total.astype(BF16)
    store(0)


def combine(load, made, store, smem):
    target, gates = load(0)[...], load(1)[...]
    tokens = load(2)[...].astype(F32)
    home = load(5)
    first, second = one_hots(target, home.shape[0] * CAP)
    rows = rows_of(home, 0)
    weight = weighted(first, second, gates)
    total = tokens
    for _ in range(3):
        part = weight.astype(BF16)
        weight = weight - part.astype(F32)
        total = total + lax.dot_general(part, rows, TN, preferred_element_type=F32)
    made[0][...] = total.astype(BF16)
    store(0)
    back = lax.dot_general(either(first, second), rows_of(home, 1), TN, preferred_element_type=F32)
    scaled = back * load(3)[...][None]
    center, inv_std = load(6)[:, 0:1], load(6)[:, 1:2]
    standard = (tokens - center) * inv_std
    inner = jnp.mean(scaled * standard, axis=-1, keepdims=True)
    centred = scaled - jnp.mean(scaled, axis=-1, keepdims=True) - standard * inner
    made[1][...] = (load(4)[...].astype(F32) + inv_std * centred).astype(BF16)
    store(1)


def on_device(n_dp, tokens, upstream, gates, expert, slot, kept, counts, gain, bias, in_weight, out_weight):
    experts = counts.shape[1]
    slots = experts * CAP
    n_tok, features = tokens.shape
    in_a, out_a = in_weight[0], out_weight[0]
    hidden = in_a.shape[1]
    half = experts // 2
    n_rows = slots * n_dp // 2
    right = [(i, (i + 2) % n_dp) for i in range(n_dp)]
    left = [(i, (i - 2) % n_dp) for i in range(n_dp)]
    sibling = [(i, i ^ 1) for i in range(n_dp)]

    def send(array, pairs):
        return lax.ppermute(array, "dp", pairs)

    def exchange(rows):
        return lax.all_to_all(rows, "expert", 0, 0, tiled=True)

    def add(a, b):
        return (a.astype(F32) + b.astype(F32)).astype(BF16)

    gates_t, expert_t, slot_t, kept_t = gates.T, expert.T, slot.T, kept.T
    block = sds((experts, 2, CAP, features), BF16)
    half_block = sds((half, 2, CAP, features), BF16)
    small = 2 * slots * n_tok * features
    rows, target, stats = call(
        dispatch,
        [block, sds((2, n_tok), jnp.int32), sds((n_tok, 2), F32)],
        [expert_t, slot_t, kept_t, gates_t, upstream, tokens, gain, bias],
        scalars=[counts],
        keep=range(3),
        flops=2 * small,
        name="dispatch",
    )
    in_b, out_b = after((in_a, out_a), target)
    in_b, out_b = send(in_b, sibling), send(out_b, sibling)
    rows, in_b, out_b = lax.optimization_barrier((exchange(rows), in_b, out_b))
    top, bottom = rows[:half], rows[half:]
    near = send(top, left), send(bottom, left), send(top, right), send(bottom, right)

    def experts_of(blocks, results, name):
        n = sum(b.shape[0] for b in blocks) * CAP
        wide, narrow = sds((n, features), BF16), sds((n, hidden), BF16)
        return call(
            functools.partial(expert_rows, len(blocks)),
            [wide, wide] + [narrow] * 4 + results,
            [*blocks, in_a, out_a, in_b, out_b],
            here=range(len(blocks) + 4),
            keep=range(6, 6 + len(results)),
            flops=16 * n * features * hidden,
            name=name,
        )

    own_block = sds(block.shape, F32)
    x_own, g_own, own_act_a, own_act_b, own_grad_a, own_grad_b, own = experts_of([rows], [own_block], "own_rows")
    far_top, far_bottom = send(near[0], left), send(near[3], right)
    near, own = lax.optimization_barrier((near, own))
    x_near, g_near, act_a, act_b, grad_a, grad_b, right_top, right_bottom, left_top, left_bottom = experts_of(
        near, [half_block] * 4, "near_rows"
    )
    far_top, far_bottom = after((far_top, far_bottom), right_bottom, left_top)
    right_bottom, left_top = send(right_bottom, right), send(left_top, left)
    x_far, g_far, far_act_a, far_act_b, far_grad_a, far_grad_b, far_top, far_bottom = experts_of(
        [far_top, far_bottom], [half_block] * 2, "far_rows"
    )
    far_top, far_bottom = send(far_top, right), send(far_bottom, left)
    first, second = sds(in_a.shape, BF16), sds(out_a.shape, BF16)
    flops = 4 * n_rows * features * hidden
    first_b, second_b = call(
        weight_grads,
        [first, second],
        after([x_near, grad_b], right_bottom, left_top)
        + [x_far, far_grad_b, x_own, own_grad_b, act_b, g_near, far_act_b, g_far, own_act_b, g_own],
        keep=range(2),
        flops=flops,
        name="weights_b",
    )
    right_top, left_bottom, first_b, second_b = lax.optimization_barrier(
        (add(right_top, far_top), add(left_bottom, far_bottom), first_b, second_b)
    )
    right_top, left_bottom = send(right_top, right), send(left_bottom, left)
    more_first, more_second = send(first_b, sibling), send(second_b, sibling)
    parts = [own, right_top, right_bottom, left_top, left_bottom]
    (home,) = call(home_sum, [block], parts, here=range(5), keep=[0], name="home_sum")
    home = exchange(home)
    grad_first, grad_second = call(
        weight_sums,
        [first, second],
        [x_near, grad_a, x_far, far_grad_a, x_own, own_grad_a]
        + [act_a, g_near, far_act_a, g_far, own_act_a, g_own, more_first, more_second],
        here=(12, 13),
        flops=flops,
        name="weights_a",
    )
    home = after(home, grad_first)
    like = sds(tokens.shape, BF16)
    mixed, grad_in = call(
        combine,
        [like, like],
        [target, gates_t, tokens, gain, upstream, home, stats],
        here=range(7),
        flops=4 * small,
        name="combine",
    )
    return mixed, grad_in, grad_first[None], grad_second[None]


def solution(mesh):
    rows = P(("expert", "dp"), None)
    in_specs = (rows,) * 7 + (P(), P(), P("expert", None, "dp"), P("expert", "dp", None))
    out_specs = (rows, rows, P("expert", None, "dp"), P("expert", "dp", None))
    body = functools.partial(on_device, mesh.shape["dp"])
    return jax.shard_map(body, mesh=mesh, in_specs=in_specs, out_specs=out_specs, check_vma=False)
```

```python
import functools

import jax
import jax.numpy as jnp
from jax import lax
from jax.experimental import pallas as pl
from jax.experimental.pallas import tpu as pltpu
from jax.sharding import PartitionSpec as P

CAP = 4
EPSILON = 1e-06
HBM = pl.BlockSpec(memory_space=pltpu.HBM)
VMEM = pl.BlockSpec(memory_space=pltpu.VMEM)
MIB = 1024 * 1024
F32 = jnp.float32
BF16 = jnp.bfloat16
TN = (((0,), (0,)), ((), ()))
NT = (((1,), (1,)), ((), ()))
sds = jax.ShapeDtypeStruct


def call(body, outs, ins, scalars=(), here=(), keep=(), flops=0, name=None):
    n_in, n_out, n_s = len(ins), len(outs), len(scalars)
    ins = [list(a) if isinstance(a, (list, tuple)) else [a] for a in ins]
    flat_in = [a for group in ins for a in group]
    first = [sum(len(g) for g in ins[:i]) for i in range(n_in)]
    far_in = [i for i in range(n_in) if i not in here]
    far_out = [i for i in range(n_out) if i not in keep]

    def kernel(*refs):
        words, refs = refs[:n_s], refs[n_s:]
        source, refs = refs[: len(flat_in)], refs[len(flat_in) :]
        sink, refs = refs[:n_out], refs[n_out:]
        held, refs = dict(zip(far_in, refs)), refs[len(far_in) :]
        made, refs = dict(zip(far_out, refs)), refs[len(far_out) :]
        in_sem, out_sem, word_sem, *smem = refs
        word_copies = [pltpu.make_async_copy(a, b, word_sem.at[k]) for k, (a, b) in enumerate(zip(words, smem))]
        copies = {}
        for i in far_in:
            at, copies[i] = 0, []
            for k in range(first[i], first[i] + len(ins[i])):
                n = flat_in[k].shape[0]
                target = held[i] if len(ins[i]) == 1 else held[i].at[pl.ds(at, n)]
                copies[i].append(pltpu.make_async_copy(source[k], target, in_sem.at[k]))
                at += n
        for c in word_copies + [c for group in copies.values() for c in group]:
            c.start()
        for c in word_copies:
            c.wait()
        waited, sent = set(), []

        def load(i):
            if i not in copies:
                return source[first[i]]
            if i not in waited:
                waited.add(i)
                for c in copies[i]:
                    c.wait()
            return held[i]

        def store(i):
            if i in made:
                c = pltpu.make_async_copy(made[i], sink[i], out_sem.at[far_out.index(i)])
                c.start()
                sent.append(c)

        body(load, [made.get(i, sink[i]) for i in range(n_out)], store, smem)
        for c in sent:
            c.wait()

    moved = sum(a.size * a.dtype.itemsize for a in list(outs) + flat_in)
    buffers = [pltpu.VMEM((sum(a.shape[0] for a in ins[i]),) + ins[i][0].shape[1:], ins[i][0].dtype) for i in far_in]
    buffers += [pltpu.VMEM(outs[i].shape, outs[i].dtype) for i in far_out]
    sems = [pltpu.SemaphoreType.DMA((max(1, k),)) for k in (len(flat_in), len(far_out), n_s)]
    smem_words = [pltpu.SMEM(a.shape, a.dtype) for a in scalars]
    scalars = [pltpu.with_memory_space_constraint(a, pltpu.HBM) for a in scalars]
    given, specs = [], [HBM] * n_s
    for i, group in enumerate(ins):
        for a in group:
            given.append(a if i in here else pltpu.with_memory_space_constraint(a, pltpu.HBM))
            specs.append(VMEM if i in here else HBM)
    outs = [o if i in keep else pltpu.HBM(o.shape, o.dtype) for i, o in enumerate(outs)]
    return pl.pallas_call(
        kernel,
        out_shape=outs,
        in_specs=specs,
        out_specs=[VMEM if i in keep else HBM for i in range(n_out)],
        scratch_shapes=buffers + sems + smem_words,
        compiler_params=pltpu.CompilerParams(vmem_limit_bytes=28 * MIB),
        cost_estimate=pl.CostEstimate(flops=flops, bytes_accessed=moved, transcendentals=0),
        name=name,
    )(*scalars, *given)


def after(values, *others):
    return lax.optimization_barrier((values, others))[0]


def moments(floats):
    center = jnp.mean(floats, axis=-1, keepdims=True)
    spread = jnp.mean(jnp.square(floats - center), axis=-1, keepdims=True)
    return center, lax.rsqrt(spread + EPSILON)


def one_hots(target, rows, part):
    row = lax.broadcasted_iota(jnp.int32, (rows, target.shape[1]), 0)
    slot = jnp.where(row // CAP % 2 == part, row // (2 * CAP) * CAP + row % CAP, -1)
    return slot == target[0:1], slot == target[1:2]


def travelling(index, rows):
    part = jnp.where(index < rows // 2, 0, 1)
    i = index - part * (rows // 2)
    return i // CAP * (2 * CAP) + part * CAP + i % CAP


def permutation(rows, apart):
    down = lax.broadcasted_iota(jnp.int32, (rows, rows), 0)
    across = lax.broadcasted_iota(jnp.int32, (rows, rows), 1)
    here = travelling(down, rows) == across if apart else travelling(across, rows) == down
    return jnp.where(here, 1.0, 0.0).astype(BF16)


def either(first, second):
    return jnp.where(first | second, 1.0, 0.0).astype(BF16)


def weighted(first, second, gates):
    return jnp.where(first, gates[0:1], 0.0) + jnp.where(second, gates[1:2], 0.0)


def dispatch(load, made, store, smem):
    (counts,) = smem
    experts = counts.shape[1]
    slots = experts * CAP
    chosen, slot, kept = load(0)[...], load(1)[...], load(2)[...]
    allowed = jnp.zeros(chosen.shape, jnp.int32)
    for e in range(experts):
        allowed = jnp.where(chosen == e, counts[0, e], allowed)
    active = (kept == 1) & (slot < allowed)
    target = jnp.where(active, chosen * CAP + slot, slots)
    made[1][...] = target
    store(1)
    rows = made[0].shape[0]
    first, second = one_hots(target, rows, 1)
    gate = jnp.sum(weighted(first, second, load(3)[...]), axis=1, keepdims=True)
    total = gate * jnp.dot(either(first, second), load(4)[...], preferred_element_type=F32)
    floats = load(5)[...].astype(F32)
    center, inv_std = moments(floats)
    made[2][:, 0:1] = center
    made[2][:, 1:2] = inv_std
    normed = ((floats - center) * inv_std * load(6)[...][None] + load(7)[...][None]).astype(BF16)
    pick = either(*one_hots(target, rows, 0))
    total = total + jnp.dot(pick, normed, preferred_element_type=F32)
    made[0][...] = total.astype(BF16)


def expert_rows(n, load, made, store, smem):
    x_all, g_all = made[0], made[1]
    at = 0
    for i in range(n):
        block = load(i)[...]
        rows = block.shape[0]
        kinds = jnp.dot(permutation(rows, True), block, preferred_element_type=F32).astype(BF16)
        x_all[pl.ds(at, rows // 2), :] = kinds[: rows // 2]
        g_all[pl.ds(at, rows // 2), :] = kinds[rows // 2 :]
        at += rows // 2
    store(0)
    store(1)
    c = 0.7978845608028654
    out, back = None, None
    for k in range(2):
        w_in, w_out = load(n + 2 * k), load(n + 2 * k + 1)
        v = jnp.dot(x_all[...], w_in[...], preferred_element_type=F32)
        square = v * v
        t = jnp.tanh(c * v * (1.0 + 0.044715 * square))
        act, grad = made[2 + k], made[4 + k]
        act[...] = (0.5 * v * (1.0 + t)).astype(BF16)
        store(2 + k)
        slope = 0.5 * (1.0 + t) + 0.5 * v * (1.0 - t * t) * (c * (1.0 + 3 * 0.044715 * square))
        hidden = lax.dot_general(g_all[...], w_out[...], NT, preferred_element_type=F32)
        grad[...] = (hidden * slope).astype(BF16)
        store(4 + k)
        term = jnp.dot(act[...], w_out[...], preferred_element_type=F32)
        out = term if out is None else out + term
        term = lax.dot_general(grad[...], w_in[...], NT, preferred_element_type=F32)
        back = term if back is None else back + term
    out, back = out.astype(BF16), back.astype(BF16)
    at = 0
    for i in range(6, len(made)):
        rows = made[i].shape[0]
        kinds = jnp.concatenate([out[at : at + rows // 2], back[at : at + rows // 2]], 0)
        made[i][...] = jnp.dot(permutation(rows, False), kinds, preferred_element_type=F32).astype(BF16)
        at += rows // 2


def weight_grads(load, made, store, smem):
    for k in range(2):
        total = lax.dot_general(load(2 * k)[...], load(2 * k + 1)[...], TN, preferred_element_type=F32)
        made[k][...] = total.astype(BF16)
        store(k)


def weight_sums(load, made, store, smem):
    for k in range(2):
        total = lax.dot_general(load(2 * k)[...], load(2 * k + 1)[...], TN, preferred_element_type=F32)
        made[k][...] = (total + load(4 + k)[...].astype(F32)).astype(BF16)
        store(k)


def home_sum(load, made, store, smem):
    half = made[0].shape[0] // 2
    for k in range(2):
        part = pl.ds(k * half, half)
        total = load(0)[part, :].astype(F32) + load(1 + k)[...].astype(F32) + load(3 + k)[...].astype(F32)
        made[0][part, :] = total.astype(BF16)
    store(0)


def combine(load, made, store, smem):
    target, gates = load(0)[...], load(1)[...]
    tokens = load(2)[...].astype(F32)
    home = load(5)
    rows = home[...]
    weight = weighted(*one_hots(target, rows.shape[0], 0), gates)
    total = tokens
    for _ in range(3):
        part = weight.astype(BF16)
        weight = weight - part.astype(F32)
        total = total + lax.dot_general(part, rows, TN, preferred_element_type=F32)
    made[0][...] = total.astype(BF16)
    store(0)
    pick = either(*one_hots(target, rows.shape[0], 1))
    back = lax.dot_general(pick, rows, TN, preferred_element_type=F32)
    scaled = back * load(3)[...][None]
    center, inv_std = load(6)[:, 0:1], load(6)[:, 1:2]
    standard = (tokens - center) * inv_std
    inner = jnp.mean(scaled * standard, axis=-1, keepdims=True)
    centred = scaled - jnp.mean(scaled, axis=-1, keepdims=True) - standard * inner
    made[1][...] = (load(4)[...].astype(F32) + inv_std * centred).astype(BF16)
    store(1)


def on_device(n_dp, tokens, upstream, gates, expert, slot, kept, counts, gain, bias, in_weight, out_weight):
    experts = counts.shape[1]
    slots = experts * CAP
    n_tok, features = tokens.shape
    in_a, out_a = in_weight[0], out_weight[0]
    hidden = in_a.shape[1]
    half = slots
    n_rows = slots * n_dp // 2
    right = [(i, (i + 2) % n_dp) for i in range(n_dp)]
    left = [(i, (i - 2) % n_dp) for i in range(n_dp)]
    sibling = [(i, i ^ 1) for i in range(n_dp)]

    def send(array, pairs):
        return lax.ppermute(array, "dp", pairs)

    def exchange(rows):
        rows = rows.reshape(experts, 2 * CAP, features)
        return lax.all_to_all(rows, "expert", 0, 0, tiled=True).reshape(2 * slots, features)

    def add(a, b):
        return (a.astype(F32) + b.astype(F32)).astype(BF16)

    gates_t, expert_t, slot_t, kept_t = gates.T, expert.T, slot.T, kept.T
    block = sds((2 * slots, features), BF16)
    half_block = sds((half, features), BF16)
    small = 2 * slots * n_tok * features
    rows, target, stats = call(
        dispatch,
        [block, sds((2, n_tok), jnp.int32), sds((n_tok, 2), F32)],
        [expert_t, slot_t, kept_t, gates_t, upstream, tokens, gain, bias],
        scalars=[counts],
        keep=range(3),
        flops=2 * small,
        name="dispatch",
    )
    in_b, out_b = send(in_a, sibling), send(out_a, sibling)
    rows, in_b, out_b = lax.optimization_barrier((exchange(rows), in_b, out_b))
    top, bottom = rows[:half], rows[half:]
    near = send(top, left), send(bottom, left), send(top, right), send(bottom, right)

    def experts_of(blocks, results, name):
        n = sum(b.shape[0] for b in blocks) // 2
        wide, narrow = sds((n, features), BF16), sds((n, hidden), BF16)
        return call(
            functools.partial(expert_rows, len(blocks)),
            [wide, wide] + [narrow] * 4 + results,
            [*blocks, in_a, out_a, in_b, out_b],
            here=range(len(blocks) + 4),
            keep=range(6, 6 + len(results)),
            flops=16 * n * features * hidden,
            name=name,
        )

    x_own, g_own, own_act_a, own_act_b, own_grad_a, own_grad_b, own = experts_of([rows], [block], "own_rows")
    far_top, far_bottom = send(near[0], left), send(near[3], right)
    near, own = lax.optimization_barrier((near, own))
    x_near, g_near, act_a, act_b, grad_a, grad_b, right_top, right_bottom, left_top, left_bottom = experts_of(
        near, [half_block] * 4, "near_rows"
    )
    far_top, far_bottom = after((far_top, far_bottom), right_bottom, left_top)
    right_bottom, left_top = send(right_bottom, right), send(left_top, left)
    x_far, g_far, far_act_a, far_act_b, far_grad_a, far_grad_b, far_top, far_bottom = experts_of(
        [far_top, far_bottom], [half_block] * 2, "far_rows"
    )
    far_top, far_bottom = send(far_top, right), send(far_bottom, left)
    first, second = sds(in_a.shape, BF16), sds(out_a.shape, BF16)
    flops = 4 * n_rows * features * hidden
    x_near, grad_b = after((x_near, grad_b), right_bottom, left_top)
    x_all, g_all = [x_near, x_far, x_own], [g_near, g_far, g_own]
    act_b, grad_b = [act_b, far_act_b, own_act_b], [grad_b, far_grad_b, own_grad_b]
    act_a, grad_a = [act_a, far_act_a, own_act_a], [grad_a, far_grad_a, own_grad_a]
    first_b, second_b = call(
        weight_grads, [first, second], [x_all, grad_b, act_b, g_all], keep=range(2), flops=flops, name="weights_b"
    )
    right_top, left_bottom, first_b, second_b = lax.optimization_barrier(
        (add(right_top, far_top), add(left_bottom, far_bottom), first_b, second_b)
    )
    right_top, left_bottom = send(right_top, right), send(left_bottom, left)
    more_first, more_second = send(first_b, sibling), send(second_b, sibling)
    parts = [own, right_top, right_bottom, left_top, left_bottom]
    (home,) = call(home_sum, [block], parts, here=range(5), keep=[0], name="home_sum")
    home = exchange(home)
    grad_first, grad_second = call(
        weight_sums,
        [first, second],
        [x_all, grad_a, act_a, g_all, more_first, more_second],
        here=(4, 5),
        flops=flops,
        name="weights_a",
    )
    home = after(home, grad_first)
    like = sds(tokens.shape, BF16)
    mixed, grad_in = call(
        combine,
        [like, like],
        [target, gates_t, tokens, gain, upstream, home, stats],
        here=range(7),
        flops=4 * small,
        name="combine",
    )
    return mixed, grad_in, grad_first[None], grad_second[None]


def solution(mesh):
    rows = P(("expert", "dp"), None)
    in_specs = (rows,) * 7 + (P(), P(), P("expert", None, "dp"), P("expert", "dp", None))
    out_specs = (rows, rows, P("expert", None, "dp"), P("expert", "dp", None))
    body = functools.partial(on_device, mesh.shape["dp"])
    return jax.shard_map(body, mesh=mesh, in_specs=in_specs, out_specs=out_specs, check_vma=False)
```

```python
import functools

import jax
import jax.numpy as jnp
from jax import lax
from jax.experimental import pallas as pl
from jax.experimental.pallas import tpu as pltpu
from jax.sharding import PartitionSpec as P

CAP = 4
EPSILON = 1e-06
HBM = pl.BlockSpec(memory_space=pltpu.HBM)
VMEM = pl.BlockSpec(memory_space=pltpu.VMEM)
MIB = 1024 * 1024
F32 = jnp.float32
BF16 = jnp.bfloat16
TN = (((0,), (0,)), ((), ()))
NT = (((1,), (1,)), ((), ()))
sds = jax.ShapeDtypeStruct


def call(body, outs, ins, scalars=(), here=(), keep=(), flops=0, name=None):
    n_in, n_out, n_s = len(ins), len(outs), len(scalars)
    ins = [list(a) if isinstance(a, (list, tuple)) else [a] for a in ins]
    flat_in = [a for group in ins for a in group]
    first = [sum(len(g) for g in ins[:i]) for i in range(n_in)]
    far_in = [i for i in range(n_in) if i not in here]
    far_out = [i for i in range(n_out) if i not in keep]

    def kernel(*refs):
        words, refs = refs[:n_s], refs[n_s:]
        source, refs = refs[: len(flat_in)], refs[len(flat_in) :]
        sink, refs = refs[:n_out], refs[n_out:]
        held, refs = dict(zip(far_in, refs)), refs[len(far_in) :]
        made, refs = dict(zip(far_out, refs)), refs[len(far_out) :]
        in_sem, out_sem, word_sem, *smem = refs
        word_copies = [pltpu.make_async_copy(a, b, word_sem.at[k]) for k, (a, b) in enumerate(zip(words, smem))]
        copies = {}
        for i in far_in:
            at, copies[i] = 0, []
            for k in range(first[i], first[i] + len(ins[i])):
                n = flat_in[k].shape[0]
                target = held[i] if len(ins[i]) == 1 else held[i].at[pl.ds(at, n)]
                copies[i].append(pltpu.make_async_copy(source[k], target, in_sem.at[k]))
                at += n
        for c in word_copies + [c for group in copies.values() for c in group]:
            c.start()
        for c in word_copies:
            c.wait()
        waited, sent = set(), []

        def load(i):
            if i not in copies:
                return source[first[i]]
            if i not in waited:
                waited.add(i)
                for c in copies[i]:
                    c.wait()
            return held[i]

        def store(i):
            if i in made:
                c = pltpu.make_async_copy(made[i], sink[i], out_sem.at[far_out.index(i)])
                c.start()
                sent.append(c)

        body(load, [made.get(i, sink[i]) for i in range(n_out)], store, smem)
        for c in sent:
            c.wait()

    moved = sum(a.size * a.dtype.itemsize for a in list(outs) + flat_in)
    buffers = [pltpu.VMEM((sum(a.shape[0] for a in ins[i]),) + ins[i][0].shape[1:], ins[i][0].dtype) for i in far_in]
    buffers += [pltpu.VMEM(outs[i].shape, outs[i].dtype) for i in far_out]
    sems = [pltpu.SemaphoreType.DMA((max(1, k),)) for k in (len(flat_in), len(far_out), n_s)]
    smem_words = [pltpu.SMEM(a.shape, a.dtype) for a in scalars]
    scalars = [pltpu.with_memory_space_constraint(a, pltpu.HBM) for a in scalars]
    given, specs = [], [HBM] * n_s
    for i, group in enumerate(ins):
        for a in group:
            given.append(a if i in here else pltpu.with_memory_space_constraint(a, pltpu.HBM))
            specs.append(VMEM if i in here else HBM)
    outs = [o if i in keep else pltpu.HBM(o.shape, o.dtype) for i, o in enumerate(outs)]
    return pl.pallas_call(
        kernel,
        out_shape=outs,
        in_specs=specs,
        out_specs=[VMEM if i in keep else HBM for i in range(n_out)],
        scratch_shapes=buffers + sems + smem_words,
        compiler_params=pltpu.CompilerParams(vmem_limit_bytes=28 * MIB),
        cost_estimate=pl.CostEstimate(flops=flops, bytes_accessed=moved, transcendentals=0),
        name=name,
    )(*scalars, *given)


def after(values, *others):
    return lax.optimization_barrier((values, others))[0]


def moments(floats):
    center = jnp.mean(floats, axis=-1, keepdims=True)
    spread = jnp.mean(jnp.square(floats - center), axis=-1, keepdims=True)
    return center, lax.rsqrt(spread + EPSILON)


def one_hots(target, slots):
    rows = lax.broadcasted_iota(jnp.int32, (slots, target.shape[1]), 0)
    return rows == target[0:1], rows == target[1:2]


def either(first, second):
    return jnp.where(first | second, 1.0, 0.0).astype(BF16)


def weighted(first, second, gates):
    return jnp.where(first, gates[0:1], 0.0) + jnp.where(second, gates[1:2], 0.0)


def rows_of(ref, part):
    return ref[:, part].reshape(ref.shape[0] * ref.shape[2], ref.shape[3])


def dispatch(load, made, store, smem):
    (counts,) = smem
    experts = counts.shape[1]
    slots = experts * CAP
    chosen, slot, kept = load(0)[...], load(1)[...], load(2)[...]
    allowed = jnp.zeros(chosen.shape, jnp.int32)
    for e in range(experts):
        allowed = jnp.where(chosen == e, counts[0, e], allowed)
    active = (kept == 1) & (slot < allowed)
    target = jnp.where(active, chosen * CAP + slot, slots)
    made[1][...] = target
    store(1)
    first, second = one_hots(target, slots)
    pick = either(first, second)
    gate = jnp.sum(weighted(first, second, load(3)[...]), axis=1, keepdims=True)
    block = (experts, CAP, made[0].shape[3])
    rows = gate * jnp.dot(pick, load(4)[...], preferred_element_type=F32)
    made[0][:, 1] = rows.astype(BF16).reshape(block)
    floats = load(5)[...].astype(F32)
    center, inv_std = moments(floats)
    made[2][:, 0:1] = center
    made[2][:, 1:2] = inv_std
    normed = ((floats - center) * inv_std * load(6)[...][None] + load(7)[...][None]).astype(BF16)
    rows = jnp.dot(pick, normed, preferred_element_type=F32)
    made[0][:, 0] = rows.astype(BF16).reshape(block)
    store(0)


def expert_rows(n, load, made, store, smem):
    x_all, g_all = made[0], made[1]
    for part, out in ((0, x_all), (1, g_all)):
        at = 0
        for i in range(n):
            rows = rows_of(load(i), part)
            out[pl.ds(at, rows.shape[0]), :] = rows
            at += rows.shape[0]
        store(part)
    c = 0.7978845608028654
    out, back = None, None
    for k in range(2):
        w_in, w_out = load(n + 2 * k), load(n + 2 * k + 1)
        v = jnp.dot(x_all[...], w_in[...], preferred_element_type=F32)
        square = v * v
        t = jnp.tanh(c * v * (1.0 + 0.044715 * square))
        act, grad = made[2 + k], made[4 + k]
        act[...] = (0.5 * v * (1.0 + t)).astype(BF16)
        store(2 + k)
        slope = 0.5 * (1.0 + t) + 0.5 * v * (1.0 - t * t) * (c * (1.0 + 3 * 0.044715 * square))
        hidden = lax.dot_general(g_all[...], w_out[...], NT, preferred_element_type=F32)
        grad[...] = (hidden * slope).astype(BF16)
        store(4 + k)
        term = jnp.dot(act[...], w_out[...], preferred_element_type=F32)
        out = term if out is None else out + term
        term = lax.dot_general(grad[...], w_in[...], NT, preferred_element_type=F32)
        back = term if back is None else back + term
    at = 0
    for i in range(6, len(made)):
        ref = made[i]
        size = ref.shape[0] * CAP
        for part, total in ((0, out), (1, back)):
            piece = total[at : at + size].astype(ref.dtype)
            ref[:, part] = piece.reshape(ref.shape[0], CAP, ref.shape[3])
        store(i)
        at += size


def weight_grads(load, made, store, smem):
    for k in range(2):
        total = lax.dot_general(load(2 * k)[...], load(2 * k + 1)[...], TN, preferred_element_type=F32)
        made[k][...] = total.astype(BF16)
        store(k)


def weight_sums(load, made, store, smem):
    for k in range(2):
        total = lax.dot_general(load(2 * k)[...], load(2 * k + 1)[...], TN, preferred_element_type=F32)
        made[k][...] = (total + load(4 + k)[...].astype(F32)).astype(BF16)
        store(k)


def home_sum(load, made, store, smem):
    half = made[0].shape[0] // 2
    for k in range(2):
        part = pl.ds(k * half, half)
        total = load(0)[part] + load(1 + k)[...].astype(F32) + load(3 + k)[...].astype(F32)
        made[0][part] = total.astype(BF16)
    store(0)


def combine(load, made, store, smem):
    target, gates = load(0)[...], load(1)[...]
    tokens = load(2)[...].astype(F32)
    home = load(5)
    first, second = one_hots(target, home.shape[0] * CAP)
    rows = rows_of(home, 0)
    weight = weighted(first, second, gates)
    total = tokens
    for _ in range(3):
        part = weight.astype(BF16)
        weight = weight - part.astype(F32)
        total = total + lax.dot_general(part, rows, TN, preferred_element_type=F32)
    made[0][...] = total.astype(BF16)
    store(0)
    back = lax.dot_general(either(first, second), rows_of(home, 1), TN, preferred_element_type=F32)
    scaled = back * load(3)[...][None]
    center, inv_std = load(6)[:, 0:1], load(6)[:, 1:2]
    standard = (tokens - center) * inv_std
    inner = jnp.mean(scaled * standard, axis=-1, keepdims=True)
    centred = scaled - jnp.mean(scaled, axis=-1, keepdims=True) - standard * inner
    made[1][...] = (load(4)[...].astype(F32) + inv_std * centred).astype(BF16)
    store(1)


def on_device(n_dp, tokens, upstream, gates, expert, slot, kept, counts, gain, bias, in_weight, out_weight):
    experts = counts.shape[1]
    slots = experts * CAP
    n_tok, features = tokens.shape
    in_a, out_a = in_weight[0], out_weight[0]
    hidden = in_a.shape[1]
    half = experts // 2
    n_rows = slots * n_dp // 2
    right = [(i, (i + 2) % n_dp) for i in range(n_dp)]
    left = [(i, (i - 2) % n_dp) for i in range(n_dp)]
    sibling = [(i, i ^ 1) for i in range(n_dp)]

    def send(array, pairs):
        return lax.ppermute(array, "dp", pairs)

    def exchange(rows):
        return lax.all_to_all(rows, "expert", 0, 0, tiled=True)

    def add(a, b):
        return (a.astype(F32) + b.astype(F32)).astype(BF16)

    gates_t, expert_t, slot_t, kept_t = gates.T, expert.T, slot.T, kept.T
    block = sds((experts, 2, CAP, features), BF16)
    half_block = sds((half, 2, CAP, features), BF16)
    small = 2 * slots * n_tok * features
    rows, target, stats = call(
        dispatch,
        [block, sds((2, n_tok), jnp.int32), sds((n_tok, 2), F32)],
        [expert_t, slot_t, kept_t, gates_t, upstream, tokens, gain, bias],
        scalars=[counts],
        keep=range(3),
        flops=2 * small,
        name="dispatch",
    )
    in_b, out_b = send(in_a, sibling), send(out_a, sibling)
    rows, in_b, out_b = lax.optimization_barrier((exchange(rows), in_b, out_b))
    top, bottom = rows[:half], rows[half:]
    near = send(top, left), send(bottom, left), send(top, right), send(bottom, right)

    def experts_of(blocks, results, name):
        n = sum(b.shape[0] for b in blocks) * CAP
        wide, narrow = sds((n, features), BF16), sds((n, hidden), BF16)
        return call(
            functools.partial(expert_rows, len(blocks)),
            [wide, wide] + [narrow] * 4 + results,
            [*blocks, in_a, out_a, in_b, out_b],
            here=range(len(blocks) + 4),
            keep=range(6, 6 + len(results)),
            flops=16 * n * features * hidden,
            name=name,
        )

    own_block = sds(block.shape, F32)
    x_own, g_own, own_act_a, own_act_b, own_grad_a, own_grad_b, own = experts_of([rows], [own_block], "own_rows")
    far_top, far_bottom = send(near[0], left), send(near[3], right)
    near, own = lax.optimization_barrier((near, own))
    x_near, g_near, act_a, act_b, grad_a, grad_b, right_top, right_bottom, left_top, left_bottom = experts_of(
        near, [half_block] * 4, "near_rows"
    )
    far_top, far_bottom = after((far_top, far_bottom), right_bottom, left_top)
    right_bottom, left_top = send(right_bottom, right), send(left_top, left)
    x_far, g_far, far_act_a, far_act_b, far_grad_a, far_grad_b, far_top, far_bottom = experts_of(
        [far_top, far_bottom], [half_block] * 2, "far_rows"
    )
    far_top, far_bottom = send(far_top, right), send(far_bottom, left)
    first, second = sds(in_a.shape, BF16), sds(out_a.shape, BF16)
    flops = 4 * n_rows * features * hidden
    x_near, grad_b = after((x_near, grad_b), right_bottom, left_top)
    x_all, g_all = [x_near, x_far, x_own], [g_near, g_far, g_own]
    act_b, grad_b = [act_b, far_act_b, own_act_b], [grad_b, far_grad_b, own_grad_b]
    act_a, grad_a = [act_a, far_act_a, own_act_a], [grad_a, far_grad_a, own_grad_a]
    first_b, second_b = call(
        weight_grads, [first, second], [x_all, grad_b, act_b, g_all], keep=range(2), flops=flops, name="weights_b"
    )
    right_top, left_bottom, first_b, second_b = lax.optimization_barrier(
        (add(right_top, far_top), add(left_bottom, far_bottom), first_b, second_b)
    )
    right_top, left_bottom = send(right_top, right), send(left_bottom, left)
    more_first, more_second = send(first_b, sibling), send(second_b, sibling)
    parts = [own, right_top, right_bottom, left_top, left_bottom]
    (home,) = call(home_sum, [block], parts, here=range(5), keep=[0], name="home_sum")
    home = exchange(home)
    grad_first, grad_second = call(
        weight_sums,
        [first, second],
        [x_all, grad_a, act_a, g_all, more_first, more_second],
        here=(4, 5),
        flops=flops,
        name="weights_a",
    )
    home = after(home, grad_first)
    like = sds(tokens.shape, BF16)
    mixed, grad_in = call(
        combine,
        [like, like],
        [target, gates_t, tokens, gain, upstream, home, stats],
        here=range(7),
        flops=4 * small,
        name="combine",
    )
    return mixed, grad_in, grad_first[None], grad_second[None]


def solution(mesh):
    rows = P(("expert", "dp"), None)
    in_specs = (rows,) * 7 + (P(), P(), P("expert", None, "dp"), P("expert", "dp", None))
    out_specs = (rows, rows, P("expert", None, "dp"), P("expert", "dp", None))
    body = functools.partial(on_device, mesh.shape["dp"])
    return jax.shard_map(body, mesh=mesh, in_specs=in_specs, out_specs=out_specs, check_vma=False)
```
